32 devices in a mesh: section: 2 (over x), dp: 16 (over z, y, core).
Axes of the slice: x: 2, y: 2, z: 4, core: 2. Of those that a mesh axis runs over, the one named last changes fastest.
Arguments:
- blocks_in: bfloat16 [2, 12288, 768], P('section', 'dp'), may hold values from -6 to 6
- gains: float32 [2, 3, 768], P('section'), may hold values from 0.5 to 1.5
- attn_qkv: bfloat16 [2, 768, 2304], P('section'), may hold values from -0.21875 to 0.21875
- attn_out: bfloat16 [2, 768, 768], P('section'), may hold values from -1.25 to 1.25
- cross_a: bfloat16 [2, 768, 768], P('section'), may hold values from -0.21875 to 0.21875
- cross_b: bfloat16 [2, 768, 768], P('section'), may hold values from -0.625 to 0.625
- mlp_in: bfloat16 [2, 768, 3072], P('section'), may hold values from -0.21875 to 0.21875
- mlp_out: bfloat16 [2, 3072, 768], P('section'), may hold values from -0.109375 to 0.109375
- lengths: int32 [2, 48, 4], P(None, 'dp'), may hold values from 0 to 256, as said below
- cotangent: float32 [2, 12288, 768], P('section', 'dp'), may hold values from -6 to 6
Outputs:
- block_out: bfloat16 [2, 12288, 768], P('section', 'dp')
- input_grad: float32 [2, 12288, 768], P('section', 'dp')
- grad_gains: float32 [2, 3, 768], P('section', None, 'dp')
- grad_attn_qkv: float32 [2, 768, 2304], P('section', 'dp')
- grad_attn_out: float32 [2, 768, 768], P('section', 'dp')
- grad_cross_a: float32 [2, 768, 768], P('section', 'dp')
- grad_cross_b: float32 [2, 768, 768], P('section', 'dp')
- grad_mlp_in: float32 [2, 768, 3072], P('section', 'dp')
- grad_mlp_out: float32 [2, 3072, 768], P('section', 'dp')
The draws below stay inside these ranges and needn't reach their ends.
Inputs may be any that keep to these rules, and one draw needn't show every extreme that they name: Samples are packed from the slot's start in order; entry j is 0 exactly when sample j is absent, and then all later entries of that slot are 0 in both rows; a present sample has 1 or more positions in both lengths[0] and lengths[1]; every slot has a sample; a slot whose first sample has 256 encoder positions (an image-text pair) holds only that sample; the entries of one slot in lengths[0] sum to at most 256, and so do those in lengths[1].
All inputs are finite; a program needn't handle non-finite values.
Results may differ from the reference program's by a relative error of at most 0.018.
Values may be sent and summed in bfloat16 or wider, within the bound.
A program may use at most 512 MiB of HBM per device.

```python
import jax
import jax.numpy as jnp
from jax import lax

D = 768
HEADS = 12
HEAD = 64
FF = 3072
ROWS = 256
SAMPLES = 4
SLOTS = 48
TOKENS = 12288


def draw_lengths(key, part):
    key = jax.random.fold_in(key, 11)
    keys = jax.random.split(key, 4)
    column = jnp.arange(SAMPLES, dtype=jnp.int32)
    first = jnp.arange(SLOTS, dtype=jnp.int32) == 0
    sample_count = jax.random.randint(keys[0], (SLOTS,), 1, SAMPLES + 1)
    sample_count = jnp.where(first, 1, sample_count)
    text_enc = jax.random.randint(keys[1], (SLOTS, SAMPLES), ROWS // 8, ROWS // SAMPLES + 1)
    text_dec = jax.random.randint(keys[2], (SLOTS, SAMPLES), ROWS // 8, ROWS // SAMPLES + 1)
    image_dec = jax.random.randint(keys[3], (SLOTS,), ROWS // 2, ROWS + 1)
    image_dec = jnp.where(first, ROWS, image_dec)
    live = column[None, :] < sample_count[:, None]
    single = (sample_count == 1)[:, None]
    lead = (column == 0)[None, :]
    enc_part = jnp.where(single, jnp.where(lead, ROWS, 0), jnp.where(live, text_enc, 0))
    dec_part = jnp.where(single, jnp.where(lead, image_dec[:, None], 0), jnp.where(live, text_dec, 0))
    return jnp.stack([enc_part, dec_part]).astype(jnp.int32)


def block_scale(rng, shape, pieces, least, largest):
    level = 1.0
    for position, shards_of in pieces:
        draws = jax.random.uniform(jax.random.fold_in(jax.random.fold_in(rng, 6), position), (shards_of,), jnp.float32, least / len(pieces), largest / len(pieces))
        level = level * jnp.repeat(jnp.exp(draws), shape[position] // shards_of).reshape((-1,) + (1,) * (len(shape) - 1 - position))
    return level


def normal_values(stream_key, dims, deviation, most, pieces=(), held_as=jnp.bfloat16):
    entries = deviation * jax.random.normal(stream_key, dims, jnp.float32)
    if pieces:
        entries = entries * block_scale(stream_key, dims, pieces, -0.22, 0.18)
    return jnp.clip(entries, -most, most).astype(held_as)


def setup_inputs(seed: int = 0) -> dict:
    arg_keys = jax.random.split(jax.random.key(seed), 11)
    return {
        "blocks_in": normal_values(arg_keys[0], (2, TOKENS, D), 1.0, 6.0, ((0, 2), (1, 16))),
        "gains": jnp.clip(1.0 + 0.1 * jax.random.normal(arg_keys[1], (2, 3, D), jnp.float32), 0.5, 1.5),
        "attn_qkv": normal_values(arg_keys[2], (2, D, 3 * D), D ** -0.5, 0.21875, ((0, 2),)),
        "attn_out": normal_values(arg_keys[3], (2, D, D), (D // 32) ** -0.5, 1.25, ((0, 2),)),
        "cross_a": normal_values(arg_keys[4], (2, D, D), D ** -0.5, 0.21875, ((0, 2),)),
        "cross_b": normal_values(arg_keys[5], (2, D, D), (D // 8) ** -0.5, 0.625, ((0, 2),)),
        "mlp_in": normal_values(arg_keys[6], (2, D, FF), D ** -0.5, 0.21875, ((0, 2),)),
        "mlp_out": normal_values(arg_keys[7], (2, FF, D), FF ** -0.5, 0.109375, ((0, 2),)),
        "lengths": draw_lengths(jax.random.fold_in(arg_keys[10], 71), 0),
        "cotangent": normal_values(arg_keys[9], (2, TOKENS, D), 1.0, 6.0, ((0, 2), (1, 16)), jnp.float32),
    }


@jax.custom_vjp
def low(v):
    return lax.optimization_barrier(v.astype(jnp.bfloat16)).astype(jnp.float32)

@jax.custom_vjp
def low_back(v):
    return v

def low_keep(v):
    return (low(v), None)

def low_pass(kept, grad):
    return (grad,)

def back_keep(v):
    return (v, None)

def back_low(kept, grad):
    return (low(grad),)
low.defvjp(low_keep, low_pass)
low_back.defvjp(back_keep, back_low)
EPSILON = 1e-06
HIGHEST = lax.Precision.HIGHEST

def product(left, right):
    return jnp.dot(left, right, precision=HIGHEST)

def norm_rows(value, gain):
    centre = lax.optimization_barrier(jnp.mean(value, axis=-1, keepdims=True))
    centred = value - centre
    spread = lax.optimization_barrier(jnp.mean(centred * centred, axis=-1, keepdims=True))
    return centred * lax.rsqrt(spread + EPSILON) * gain

def segment_ids(counts):
    ends = jnp.cumsum(counts)
    places = jnp.arange(ROWS, dtype=jnp.int32)
    return lax.optimization_barrier(jnp.sum((places[:, None] >= ends[None, :]).astype(jnp.int32), axis=1))

def build_masks(counts):
    enc_seg = segment_ids(counts[0])
    dec_seg = segment_ids(counts[1])
    places = jnp.arange(ROWS, dtype=jnp.int32)
    enc_mask = enc_seg[:, None] == enc_seg[None, :]
    dec_mask = (dec_seg[:, None] == dec_seg[None, :]) & (places[None, :] <= places[:, None])
    cross_mask = (dec_seg[:, None] == enc_seg[None, :]) | (dec_seg[:, None] == SAMPLES)
    return (enc_mask, dec_mask, cross_mask)

def attend(queries, keys, values, allowed):
    count_q = queries.shape[0]
    heads_q = queries.reshape(count_q, HEADS, HEAD)
    heads_k = keys.reshape(keys.shape[0], HEADS, HEAD)
    heads_v = values.reshape(values.shape[0], HEADS, HEAD)
    scores = low_back(jnp.einsum('qhd,khd->hqk', heads_q, heads_k, precision=HIGHEST)) * HEAD ** (-0.5)
    scores = jnp.where(allowed[None], scores, -1e+30)
    peak = lax.optimization_barrier(jnp.max(scores, axis=-1, keepdims=True))
    raised = jnp.exp(scores - peak)
    probs = raised / lax.optimization_barrier(jnp.sum(raised, axis=-1, keepdims=True))
    mixed = jnp.einsum('hqk,khd->qhd', low(probs), heads_v, precision=HIGHEST)
    return low(low_back(mixed.reshape(count_q, D)))

def self_block(value, gain, w_qkv, w_out, allowed):
    normed = low(norm_rows(value, gain))
    packed = low(low_back(product(normed, w_qkv)))
    mixed = attend(packed[:, :D], packed[:, D:2 * D], packed[:, 2 * D:], allowed)
    return value + low_back(product(mixed, w_out))

def feed_block(value, gain, w_in, w_mlp):
    normed = low(norm_rows(value, gain))
    active = low(jax.nn.gelu(low_back(product(normed, w_in)), approximate=False))
    return value + low_back(product(active, w_mlp))

def slot_forward(params, enc_in, dec_in, counts):
    gain_all, qkv_all, out_all, cra_all, crb_all, in_all, mlp_all = params
    enc_mask, dec_mask, cross_mask = build_masks(counts)
    middle = self_block(enc_in, gain_all[0, 0], qkv_all[0], out_all[0], enc_mask)
    enc_top = feed_block(middle, gain_all[0, 1], in_all[0], mlp_all[0])
    memory = low(norm_rows(enc_top, gain_all[0, 2]))
    mem_keys = low(low_back(product(memory, cra_all[0])))
    mem_values = low(low_back(product(memory, crb_all[0])))
    first = self_block(dec_in, gain_all[1, 0], qkv_all[1], out_all[1], dec_mask)
    cross_in = low(norm_rows(first, gain_all[1, 1]))
    queries = low(low_back(product(cross_in, cra_all[1])))
    second = first + low_back(product(attend(queries, mem_keys, mem_values, cross_mask), crb_all[1]))
    dec_top = feed_block(second, gain_all[1, 2], in_all[1], mlp_all[1])
    return (enc_top, dec_top)

def reference(blocks_in, gains, attn_qkv, attn_out, cross_a, cross_b, mlp_in, mlp_out, lengths, cotangent):
    params = tuple((w.astype(jnp.float32) for w in (gains, attn_qkv, attn_out, cross_a, cross_b, mlp_in, mlp_out)))
    inputs = blocks_in.astype(jnp.float32).reshape(2, SLOTS, ROWS, D)
    cotans = cotangent.astype(jnp.float32).reshape(2, SLOTS, ROWS, D)
    counts_all = jnp.transpose(lengths, (1, 0, 2))

    def one_slot(totals, item):
        enc_in, dec_in, enc_cot, dec_cot, counts = item
        outputs, pull = jax.vjp(lambda p, a, b: slot_forward(p, a, b, counts), params, enc_in, dec_in)
        grad_params, grad_enc, grad_dec = pull((enc_cot, dec_cot))
        totals = jax.tree.map(lambda s, g: s + g, totals, grad_params)
        return (totals, (outputs[0], outputs[1], grad_enc, grad_dec))
    zeros = jax.tree.map(jnp.zeros_like, params)
    grads, (enc_out, dec_out, grad_enc, grad_dec) = lax.scan(one_slot, zeros, (inputs[0], inputs[1], cotans[0], cotans[1], counts_all))
    block_out = jnp.stack([enc_out, dec_out]).reshape(2, SLOTS * ROWS, D).astype(jnp.bfloat16)
    input_grad = jnp.stack([grad_enc, grad_dec]).reshape(2, SLOTS * ROWS, D)
    return (block_out, input_grad, grads[0], grads[1], grads[2], grads[3], grads[4], grads[5], grads[6])
```

```python
import functools
import jax
import jax.numpy as jnp
from jax import lax
from jax.experimental import pallas as pl
from jax.experimental.pallas import tpu as pltpu
from jax.sharding import PartitionSpec as P

D = 768
HEADS = 12
HEAD = 64
FF = 3072
ROWS = 256
SAMPLES = 4
PAIR = 2 * HEAD
PAIRS = HEADS // 2
PIECE = ROWS // 2
WIDE = FF // D
EPSILON = 1e-06
MESH = pl.DeviceIdType.MESH
BF = jnp.bfloat16
F32 = jnp.float32

U_A, U_B, U_IN, U_OUT, U_O, U_QKV = 0, 1, 2, 6, 10, 11
UNITS = 14
RING = 4
MID_LAG = 1
LAG = 2
WINDOW, LAST_WINDOW = 4, 2
NZ, NY, NC = 4, 2, 2
SHARE = D // (NZ * NY * NC)

NAMES = ("x_h", "gains", "wqkv_h", "wo_h", "wa_h", "wb_h", "win_h", "wout_h", "lens", "cot_h")
NAMES += ("bo_h", "ig_h", "gg_out", "og_h")
NAMES += ("wqkv", "wo", "wa", "wb", "win", "wout", "res", "cot", "hid", "qkv", "mix", "up", "act")
NAMES += ("mem", "qc", "oc", "low_ff", "low_sa", "rstd", "bias")
NAMES += ("core_in", "ring", "stage", "gsum", "load_sem", "out_sem", "x_send", "x_recv")
NAMES += ("c_send", "c_recv", "y_send", "y_recv", "z_send", "z_recv", "g_send", "g_recv")
NAMES += ("stage_sem", "ready")


def nn(left, right):
    return jnp.dot(left, right, preferred_element_type=F32)


def nt(left, right):
    return lax.dot_general(left, right, (((1,), (1,)), ((), ())), preferred_element_type=F32)


def tn(left, right):
    return lax.dot_general(left, right, (((0,), (0,)), ((), ())), preferred_element_type=F32)


def norm_rows(value, gain):
    centre = jnp.mean(value, axis=-1, keepdims=True)
    centred = value - centre
    spread = jnp.mean(centred * centred, axis=-1, keepdims=True)
    scale = lax.rsqrt(spread + EPSILON)
    return centred * scale * gain, scale


def gelu_parts(u):
    phi = 0.5 * (1.0 + lax.erf(u * 0.7071067811865476))
    slope = phi + u * (jnp.exp(u * u * -0.5) * 0.3989422804014327)
    return u * phi, slope


def pair_halves(block):
    low = (lax.broadcasted_iota(jnp.int32, (1, PAIR), 1) < HEAD).astype(BF)
    return jnp.concatenate([block * low, block * (1 - low)], axis=0)


def pair_join(block):
    low = lax.broadcasted_iota(jnp.int32, (1, PAIR), 1) < HEAD
    half = block.shape[0] // 2
    return jnp.where(low, block[:half], block[half:])


def body_kernel(slots, scatter, *all_refs):
    r = dict(zip(NAMES, all_refs, strict=True))
    gains, lens = r["gains"], r["lens"]
    wqkv, wo, wa, wb, win, wout = (r[k] for k in ("wqkv", "wo", "wa", "wb", "win", "wout"))
    res, cot, hid, qkv, mix, up, act, mem = (
        r[k] for k in ("res", "cot", "hid", "qkv", "mix", "up", "act", "mem")
    )
    qc, oc, low_ff, low_sa, rstd, bias = (
        r[k] for k in ("qc", "oc", "low_ff", "low_sa", "rstd", "bias")
    )
    core_in, ring, stage, gsum = (r[k] for k in ("core_in", "ring", "stage", "gsum"))
    total = slots * ROWS

    sec = lax.axis_index("section")
    me = lax.axis_index("dp")
    across = (1 - sec, me)
    if scatter:
        core = lax.rem(me, NC)
        y = lax.rem(me // NC, NY)
        z = me // (NC * NY)
        sibling = (sec, me + 1 - 2 * core)
        beside = (sec, me + NC * (1 - 2 * y))
        along = [lax.rem(z + 1 + k, NZ) for k in range(NZ - 1)]
        along_ids = [(sec, other * (NC * NY) + y * NC + core) for other in along]
        high = z // 2
        is_end = jnp.logical_or(z == 0, z == NZ - 1)
        is_mid = jnp.logical_not(is_end)

        def at_z(other):
            return (sec, other * (NC * NY) + y * NC + core)
        partners = [across, sibling, beside] + along_ids
    else:
        partners = [across]

    barrier = pltpu.get_barrier_semaphore()
    for device in partners:
        pl.semaphore_signal(barrier, inc=1, device_id=device, device_id_type=MESH)
    pl.semaphore_wait(barrier, len(partners))

    loads = {}

    def load(name, index, pieces):
        loads[name] = [
            pltpu.make_async_copy(src, dst, r["load_sem"].at[index + i])
            for i, (src, dst) in enumerate(pieces)
        ]

    def begin(*names):
        for name in names:
            for piece in loads[name]:
                piece.start()

    def loaded(*names):
        for name in names:
            for piece in loads[name]:
                piece.wait()

    load("x", 0, [(r["x_h"], low_ff)])
    load("wqkv", 1, [(r["wqkv_h"].at[:, pl.ds(j * D, D)], wqkv.at[j]) for j in range(3)])
    load("wo", 4, [(r["wo_h"], wo)])
    load("wa", 5, [(r["wa_h"], wa)])
    load("wb", 6, [(r["wb_h"], wb)])
    load(
        "win",
        7,
        [(r["win_h"].at[:, pl.ds(j * D, D)], win.at[pl.ds(j * D, D)]) for j in range(WIDE)],
    )
    load("wout", 7 + WIDE, [(r["wout_h"], wout)])
    load("cot", 8 + WIDE, [(r["cot_h"], cot)])
    begin("x", "wqkv", "wo")
    gsum[...] = jnp.zeros_like(gsum)

    def rows_of(s):
        return pl.ds(pl.multiple_of(s * ROWS, ROWS), ROWS)

    def cols_of(t):
        return pl.ds(t * PAIR, PAIR)

    def x_copy(kind, piece, size=PIECE):
        src, dst = ((qc, qc), (oc, oc), (mem.at[0], low_sa), (qc, qc))[kind]
        rows = pl.ds(pl.multiple_of(piece * size, size), size)
        return pltpu.make_async_remote_copy(
            src_ref=src.at[rows],
            dst_ref=dst.at[rows],
            send_sem=r["x_send"].at[kind, piece],
            recv_sem=r["x_recv"].at[kind, piece],
            device_id=across,
            device_id_type=MESH,
        )

    def segments(which, s, axis):
        places = lax.broadcasted_iota(jnp.int32, (ROWS, ROWS), axis)
        end = jnp.int32(0)
        found = jnp.zeros((ROWS, ROWS), jnp.int32)
        for j in range(SAMPLES):
            end = end + lens[s, which, j]
            found = found + jnp.where(places >= end, 1, 0)
        return found

    def self_bias(decoder, s, turned, place):
        q_axis = 1 if turned else 0
        which = 1 if decoder else 0
        keep = segments(which, s, q_axis) == segments(which, s, 1 - q_axis)
        if decoder:
            q_at = lax.broadcasted_iota(jnp.int32, (ROWS, ROWS), q_axis)
            k_at = lax.broadcasted_iota(jnp.int32, (ROWS, ROWS), 1 - q_axis)
            keep = jnp.logical_and(keep, k_at <= q_at)
        bias[place, s] = jnp.where(keep, 0.0, -1e30).astype(BF)

    def cross_bias(s, turned, place):
        q_axis = 1 if turned else 0
        q_seg = segments(1, s, q_axis)
        k_seg = segments(0, s, 1 - q_axis)
        keep = jnp.logical_or(q_seg == k_seg, q_seg == SAMPLES)
        bias[place, s] = jnp.where(keep, 0.0, -1e30).astype(BF)

    def attend_fwd(queries, keys, values, out, rows, q_rows, mask):
        for t in range(PAIRS):
            cols = cols_of(t)
            q2 = pair_halves(queries[q_rows, cols] * HEAD ** (-0.5))
            scores = nt(q2, keys[rows, cols])
            block = mask[...].astype(F32)
            scores = scores + jnp.concatenate([block, block], axis=0)
            peak = jnp.max(scores, axis=-1, keepdims=True)
            raised = jnp.exp(scores - peak)
            level = 1.0 / jnp.sum(raised, axis=-1, keepdims=True)
            mixed = nn(raised.astype(BF), values[rows, cols]) * level
            out[q_rows, cols] = pair_join(mixed).astype(BF)

    def attend_bwd(queries, keys, values, grads, rows, mask):
        for t in range(PAIRS):
            cols = cols_of(t)
            q2 = pair_halves(queries[rows, cols] * HEAD ** (-0.5))
            k2 = keys[rows, cols]
            v2 = values[rows, cols]
            scores = nt(k2, q2)
            block = mask[...].astype(F32)
            scores = scores + jnp.concatenate([block, block], axis=1)
            peak = jnp.max(scores, axis=0, keepdims=True)
            raised = jnp.exp(scores - peak)
            probs = raised * (1.0 / jnp.sum(raised, axis=0, keepdims=True))
            g2 = pair_halves(grads[rows, cols])
            g_probs = nt(v2, g2)
            g_values = nn(probs.astype(BF), g2)
            inner = jnp.sum(g_probs * probs, axis=0, keepdims=True)
            g_scores = (probs * (g_probs - inner)).astype(BF)
            g_queries = pair_join(tn(g_scores, k2)) * HEAD ** (-0.5)
            g_keys = nn(g_scores, q2)
            queries[rows, cols] = g_queries.astype(BF)
            keys[rows, cols] = g_keys.astype(BF)
            values[rows, cols] = g_values.astype(BF)

    def norm_fwd(value, index, rows):
        normed, scale = norm_rows(value, gains[index])
        normed = normed.astype(BF)
        hid[index, rows, :] = normed
        rstd[index, rows, :] = jnp.broadcast_to(scale, (ROWS, 128))
        return normed

    def norm_bwd(grad, index, rows):
        gain = gains[index]
        flat = hid[index, rows, :].astype(F32) * (1.0 / gain)
        gsum[0, pl.ds(index, 1), :] += jnp.sum(grad * flat, axis=0, keepdims=True)
        scaled = grad * gain
        first = jnp.mean(scaled, axis=-1, keepdims=True)
        second = jnp.mean(scaled * flat, axis=-1, keepdims=True)
        cot[rows, :] += (scaled - first - flat * second) * rstd[index, rows, :][:, :1]

    def self_fwd(decoder, s):
        rows = rows_of(s)
        value = low_ff[rows, :].astype(F32)
        normed = norm_fwd(value, 0, rows)
        for j in range(3):
            qkv[j, rows, :] = nn(normed, wqkv[j]).astype(BF)
        attend_fwd(qkv.at[0], qkv.at[1], qkv.at[2], mix, rows, rows, bias.at[0, s])
        res[rows, :] = low_ff[rows, :].astype(F32) + nn(mix[rows, :], wo[...])

    def feed_fwd(index, s):
        rows = rows_of(s)
        normed = norm_fwd(res[rows, :], index, rows)
        for j in range(WIDE):
            active, slope = gelu_parts(nn(normed, win[pl.ds(j * D, D), :]))
            act[j, rows, :] = active.astype(BF)
            up[j, rows, :] = slope.astype(BF)
        out = res[rows, :]
        for j in range(WIDE):
            out = out + nn(act[j, rows, :], wout[pl.ds(j * D, D), :])
        return out

    def feed_bwd(index, s):
        rows = rows_of(s)
        low = cot[rows, :].astype(BF)
        low_ff[rows, :] = low
        for j in range(WIDE):
            g_active = nt(low, wout[pl.ds(j * D, D), :])
            up[j, rows, :] = (g_active * up[j, rows, :].astype(F32)).astype(BF)
        grad = nt(up[0, rows, :], win[pl.ds(0, D), :])
        for j in range(1, WIDE):
            grad = grad + nt(up[j, rows, :], win[pl.ds(j * D, D), :])
        norm_bwd(grad, index, rows)

    def grad_out(s):
        return pltpu.make_async_copy(
            cot.at[rows_of(s)], r["ig_h"].at[rows_of(s)], r["out_sem"].at[1, s]
        )

    def self_bwd(decoder, s):
        rows = rows_of(s)
        low = cot[rows, :].astype(BF)
        low_sa[rows, :] = low
        act[0, rows, :] = nt(low, wo[...]).astype(BF)
        turned = bias.at[1 if decoder else 0, s]
        attend_bwd(qkv.at[0], qkv.at[1], qkv.at[2], act.at[0], rows, turned)
        grad = nt(qkv[0, rows, :], wqkv[0])
        for j in range(1, 3):
            grad = grad + nt(qkv[j, rows, :], wqkv[j])
        norm_bwd(grad, 0, rows)
        grad_out(s).start()

    def block_out(buffer, s):
        return pltpu.make_async_copy(
            buffer.at[rows_of(s)], r["bo_h"].at[rows_of(s)], r["out_sem"].at[0, s]
        )

    place = {}

    def slot_of(u):
        return place[u] % RING

    def core_copy(u):
        return pltpu.make_async_remote_copy(
            src_ref=ring.at[slot_of(u), 1 - core],
            dst_ref=core_in.at[u],
            send_sem=r["c_send"].at[u],
            recv_sem=r["c_recv"].at[u],
            device_id=sibling,
            device_id_type=MESH,
        )

    def y_place(u, first, count=1):
        ref, base = early.get(u, (win, u * NZ * SHARE))
        return ref.at[pl.ds(base + first * SHARE, count * SHARE)]

    def z_place(u, first, count=1):
        return wout.at[pl.ds((u * NZ + first) * SHARE, count * SHARE)]

    def y_copy(u):
        return pltpu.make_async_remote_copy(
            src_ref=core_in.at[u, 1 - y],
            dst_ref=y_place(u, 0, NZ),
            send_sem=r["y_send"].at[u],
            recv_sem=r["y_recv"].at[u],
            device_id=beside,
            device_id_type=MESH,
        )

    def z_copy(u, src, dst, send, recv, to):
        return pltpu.make_async_remote_copy(
            src_ref=src,
            dst_ref=dst,
            send_sem=r["z_send"].at[u, send],
            recv_sem=r["z_recv"].at[u, recv],
            device_id=at_z(to),
            device_id_type=MESH,
        )

    def from_end(u):
        return z_copy(u, y_place(u, 1 - high, 3), z_place(u, 0, 3), 0, 0, 1 + high)

    def to_end(u):
        return z_copy(u, y_place(u, 3 * high), z_place(u, 0), 0, 0, 3 * high)

    def to_mid(u):
        return z_copy(u, z_place(u, 1), z_place(u, 3), 1, 1, 2 - high)

    def to_far(u):
        return z_copy(u, z_place(u, 2 * (1 - high)), z_place(u, 1), 2, 1, 3 * (1 - high))

    def whole_copy(u):
        return pltpu.make_async_copy(ring.at[slot_of(u)], r["og_h"].at[u], r["c_send"].at[u])

    def claim(units):
        for u in units:
            place[u] = len(place)
            before = [v for v in place if place[v] == place[u] - RING]
            for v in before:
                if scatter:
                    core_copy(v).wait_send()
                else:
                    whole_copy(v).wait()

    def send_unit(u):
        if scatter:
            core_copy(u).start()
        else:
            whole_copy(u).start()

    def make_unit(u, left, right):
        claim([u])
        slot = slot_of(u)

        value = tn(left[...], right[...]).astype(BF)
        if scatter:
            for d in range(NZ * NY * NC):
                dz, dy, dc = d // (NY * NC), d // NC % NY, d % NC
                part = value[d * SHARE : (d + 1) * SHARE]
                ring[slot, dc, dy, pl.ds(dz * SHARE, SHARE), :] = part
        else:
            ring[slot] = value
        send_unit(u)

    def make_out_units():
        units = [U_OUT + j for j in range(WIDE)]
        claim(units)

        for j in range(WIDE):
            value = tn(act[j], low_ff[...]).astype(BF)
            if scatter:
                for d in range(NY * NC):
                    for k in range(WIDE):
                        at = (d * WIDE + k) * SHARE
                        part = value[at : at + SHARE]
                        slot = slot_of(units[k])
                        ring[slot, d % NC, d // NC, pl.ds(j * SHARE, SHARE), :] = part
            else:
                ring[slot_of(units[j])] = value
        for u in units:
            send_unit(u)

    def signal_ready(which, devices):
        for device in devices:
            pl.semaphore_signal(
                r["ready"].at[which], inc=1, device_id=device, device_id_type=MESH
            )

    def ready_signal():
        if scatter:
            signal_ready(0, [beside] + along_ids)

    def ready_wait():
        if scatter:
            pl.semaphore_wait(r["ready"].at[0], NZ)

    def core_sum(u):
        if not scatter:
            return
        core_copy(u).wait_recv()
        for h in range(NY):
            core_in[u, h] = (
                core_in[u, h].astype(F32) + ring[slot_of(u), core, h].astype(F32)
            ).astype(BF)
        summed.append(u)
        pump()

    def pump():
        while summed and len(beside_now) < window[0]:
            u = summed.pop(0)
            y_copy(u).start()
            beside_now.append(u)

    def add_into(target, other):
        target[...] = (target[...].astype(F32) + other[...].astype(F32)).astype(BF)

    def tick():
        if not scatter:
            return
        u = beside_now.pop(0)
        y_copy(u).wait_recv()
        pump()
        add_into(y_place(u, 0, NZ), core_in.at[u, y])

        @pl.when(is_end)
        def _():
            from_end(u).start()

        @pl.when(is_mid)
        def _():
            to_end(u).start()

        halfway.append(u)
        if len(halfway) > MID_LAG:
            mid_sum(halfway.pop(0))

    def mid_sum(u):
        @pl.when(is_mid)
        def _():
            from_end(u).wait_recv()
            add_into(z_place(u, 1), y_place(u, 2 - high))
            to_mid(u).start()
            add_into(z_place(u, 2 * (1 - high)), y_place(u, 3 * (1 - high)))
            to_far(u).start()

        sent.append(u)
        if len(sent) > LAG:
            z_sum(sent.pop(0))

    summed, beside_now, halfway, sent, ended = [], [], [], [], []
    early = {}
    window = [WINDOW]

    def stage_copy(u, slot):
        return pltpu.make_async_copy(stage.at[slot], r["og_h"].at[u], r["stage_sem"].at[slot])

    def z_sum(u):
        @pl.when(is_end)
        def _():
            to_end(u).wait_recv()

        to_mid(u).wait_recv()
        slot = len(ended) % 2
        if len(ended) >= 2:
            stage_copy(ended[-2], slot).wait()
        value = y_place(u, z)[...].astype(F32)
        value = value + z_place(u, jnp.where(is_end, 0, 2 * high))[...].astype(F32)
        value = value + z_place(u, jnp.where(is_end, 1, 3))[...].astype(F32)
        stage[slot] = value
        stage_copy(u, slot).start()
        ended.append(u)

    def gain_copy(step):
        source, landing, device = (
            [(0, 3, sibling), (1, 4, beside)] + [(2, 5 + k, along_ids[k]) for k in range(NZ - 1)]
        )[step]
        return pltpu.make_async_remote_copy(
            src_ref=gsum.at[source],
            dst_ref=gsum.at[landing],
            send_sem=r["g_send"].at[step],
            recv_sem=r["g_recv"].at[step],
            device_id=device,
            device_id_type=MESH,
        )

    def gain_step(step):
        if not scatter:
            return
        if step == 0:
            gain_copy(0).start()
        elif step == 1:
            gain_copy(0).wait_recv()
            gsum[1] = gsum[0] + gsum[3]
            gain_copy(1).start()
        elif step == 2:
            gain_copy(1).wait_recv()
            gsum[2] = gsum[1] + gsum[4]
            for k in range(NZ - 1):
                gain_copy(2 + k).start()
        else:
            for k in range(NZ - 1):
                gain_copy(2 + k).wait_recv()

    def gain_end():
        if not scatter:
            r["gg_out"][...] = gsum[0]
            return
        value = gsum[2]
        for k in range(NZ - 1):
            value = value + gsum[5 + k]
        r["gg_out"][...] = value

    def finish():
        window[0] = LAST_WINDOW
        while beside_now:
            tick()
        while halfway:
            mid_sum(halfway.pop(0))
        while sent:
            z_sum(sent.pop(0))
        gain_step(3)
        gain_end()
        if scatter:
            for u in place:
                if place[u] >= UNITS - RING:
                    core_copy(u).wait_send()
                y_copy(u).wait_send()

            @pl.when(is_end)
            def _():
                for u in place:
                    from_end(u).wait_send()

            @pl.when(is_mid)
            def _():
                for u in place:
                    to_end(u).wait_send()
                    to_mid(u).wait_send()
                    to_far(u).wait_send()

            for step in range(1 + 1 + NZ - 1):
                gain_copy(step).wait_send()
            for back in (2, 1):
                stage_copy(ended[-back], (len(ended) - back) % 2).wait()
        else:
            for u in place:
                if place[u] >= UNITS - RING:
                    whole_copy(u).wait()
        for s in range(slots):
            grad_out(s).wait()

    def loop(count, step):
        def run(s, carry):
            step(s)
            return carry

        lax.fori_loop(0, count, run, 0)

    def encoder():
        place.clear()
        ended.clear()
        window[0] = WINDOW

        def masks(s):
            self_bias(False, s, False, 0)
            cross_bias(s, False, 1)
            cross_bias(s, True, 2)

        loop(slots, masks)
        loaded("x", "wqkv", "wo")
        begin("win", "wout", "wa", "wb", "cot")

        def cross(s, half):
            x_copy(0, 2 * s + half).wait_recv()
            start = pl.multiple_of(s * ROWS + half * PIECE, PIECE)
            mask = bias.at[1, s, pl.ds(half * PIECE, PIECE)]
            attend_fwd(qc, mem.at[0], mem.at[1], oc, rows_of(s), pl.ds(start, PIECE), mask)
            x_copy(1, 2 * s + half).start()

        def forward(s):
            @pl.when(s < slots)
            def _():
                self_fwd(False, s)

            @pl.when(s >= 1)
            def _():
                cross(s - 1, 1)

            @pl.when(s == 0)
            def _():
                loaded("win", "wout", "wa", "wb")

            @pl.when(s < slots)
            def _():
                rows = rows_of(s)
                out = feed_fwd(1, s)
                low_ff[rows, :] = out.astype(BF)
                block_out(low_ff, s).start()
                normed = norm_fwd(out, 2, rows)
                mem[0, rows, :] = nn(normed, wa[...]).astype(BF)
                mem[1, rows, :] = nn(normed, wb[...]).astype(BF)
                cross(s, 0)

        loop(slots + 1, forward)
        loaded("cot")
        for piece in range(2 * slots):
            x_copy(1, piece).wait_send()
        if scatter:
            early[U_A] = (oc, 0)
            early[U_B] = (oc, NZ * SHARE)
            signal_ready(1, [beside])

        def backward(s):
            rows = rows_of(s)
            block_out(low_ff, s).wait()
            x_copy(2, s, ROWS).wait_recv()
            attend_bwd(qc, mem.at[0], mem.at[1], low_sa, rows, bias.at[2, s])
            x_copy(3, s, ROWS).start()

            @pl.when(s == slots - 1)
            def _():
                make_unit(U_A, hid.at[2], mem.at[0])
                make_unit(U_B, hid.at[2], mem.at[1])
                if scatter:
                    pl.semaphore_wait(r["ready"].at[1], 1)
                core_sum(U_A)
                core_sum(U_B)

            grad = nt(mem[0, rows, :], wa[...]) + nt(mem[1, rows, :], wb[...])
            norm_bwd(grad, 2, rows)
            feed_bwd(1, s)

        loop(slots, backward)
        ready_signal()
        make_unit(U_IN, hid.at[1], up.at[0])
        make_unit(U_IN + 1, hid.at[1], up.at[1])
        ready_wait()
        core_sum(U_IN)
        for j in range(2, WIDE):
            make_unit(U_IN + j, hid.at[1], up.at[j])
            core_sum(U_IN + j - 1)
        core_sum(U_IN + WIDE - 1)
        make_out_units()
        tick()
        for j in range(WIDE):
            core_sum(U_OUT + j)
        tick()
        for s in range(slots):
            self_bwd(False, s)
            tick()
            if s != 1:
                tick()
        gain_step(0)
        make_unit(U_O, mix, low_sa)
        gain_step(1)
        make_unit(U_QKV, hid.at[0], qkv.at[0])
        core_sum(U_O)
        gain_step(2)
        make_unit(U_QKV + 1, hid.at[0], qkv.at[1])
        core_sum(U_QKV)
        make_unit(U_QKV + 2, hid.at[0], qkv.at[2])
        core_sum(U_QKV + 1)
        core_sum(U_QKV + 2)
        for s in range(slots):
            x_copy(3, s, ROWS).wait_send()
        finish()

    def decoder():
        place.clear()
        ended.clear()
        window[0] = WINDOW
        early.clear()
        begin("wa")

        def masks(s):
            self_bias(True, s, False, 0)
            self_bias(True, s, True, 1)

        loop(slots, masks)
        loaded("x", "wqkv", "wo")
        begin("wb", "win", "wout", "cot")
        loaded("wa")

        def first(s):
            rows = rows_of(s)
            self_fwd(True, s)
            normed = norm_fwd(res[rows, :], 1, rows)
            qc[rows, :] = nn(normed, wa[...]).astype(BF)
            x_copy(0, s).start()

        loop(slots, first)
        pieces = 2 * slots
        for piece in range(slots - 2):
            x_copy(0, piece).wait_send()
        for piece in range(slots, pieces - 1):
            x_copy(0, piece - 2).wait_send()
            x_copy(0, piece).start()
        loaded("wb", "win", "wout", "cot")

        def second(s):
            rows = rows_of(s)
            x_copy(1, 2 * s).wait_recv()
            x_copy(1, 2 * s + 1).wait_recv()
            res[rows, :] += nn(oc[rows, :], wb[...])
            low_sa[rows, :] = feed_fwd(2, s).astype(BF)
            block_out(low_sa, s).start()

            @pl.when(s == 0)
            def _():
                x_copy(0, pieces - 3).wait_send()
                x_copy(0, pieces - 1).start()

            feed_bwd(2, s)
            low = cot[rows, :].astype(BF)
            mem[1, rows, :] = low
            mem[0, rows, :] = nt(low, wb[...]).astype(BF)

            @pl.when(s == slots - 1)
            def _():
                x_copy(0, pieces - 2).wait_send()
                x_copy(0, pieces - 1).wait_send()

            x_copy(2, s, ROWS).start()

        loop(slots, second)
        ready_signal()
        make_unit(U_IN, hid.at[2], up.at[0])
        ready_wait()
        for j in range(1, WIDE):
            make_unit(U_IN + j, hid.at[2], up.at[j])
            core_sum(U_IN + j - 1)
        core_sum(U_IN + WIDE - 1)
        make_out_units()
        tick()
        for j in range(WIDE):
            core_sum(U_OUT + j)
        make_unit(U_B, oc, mem.at[1])
        core_sum(U_B)
        tick()

        def third(s):
            rows = rows_of(s)
            x_copy(3, s, ROWS).wait_recv()
            block_out(low_sa, s).wait()
            norm_bwd(nt(qc[rows, :], wa[...]), 1, rows)
            self_bwd(True, s)

        for s in range(slots):
            third(s)
            tick()
        gain_step(0)
        make_unit(U_A, hid.at[1], qc)
        gain_step(1)
        make_unit(U_O, mix, low_sa)
        core_sum(U_A)
        gain_step(2)
        make_unit(U_QKV, hid.at[0], qkv.at[0])
        core_sum(U_O)
        make_unit(U_QKV + 1, hid.at[0], qkv.at[1])
        core_sum(U_QKV)
        make_unit(U_QKV + 2, hid.at[0], qkv.at[2])
        core_sum(U_QKV + 1)
        core_sum(U_QKV + 2)
        for s in range(slots):
            x_copy(2, s, ROWS).wait_send()
        finish()

    @pl.when(sec == 0)
    def _():
        encoder()

    @pl.when(sec == 1)
    def _():
        decoder()


def results_kernel(out, grad, gain, units, o_out, o_grad, o_gain, *rest):
    o_grads = rest[:6]
    v_out, v_grad, v_units, in_sem, sem = rest[6:]
    coming = [
        pltpu.make_async_copy(a, b, in_sem.at[i])
        for i, (a, b) in enumerate(((out, v_out), (grad, v_grad), (units, v_units)))
    ]
    for copy in coming:
        copy.start()
    steps = [(v_out, o_out, 0), (v_grad, o_grad, 1)]
    o_qkv, o_o, o_a, o_b, o_in, o_mlp = o_grads
    for target, first, count in ((o_qkv, U_QKV, 3), (o_in, U_IN, WIDE)):
        for j in range(count):
            steps.append((v_units.at[first + j], target.at[:, pl.ds(j * D, D)], 2))
    for target, u in ((o_o, U_O), (o_a, U_A), (o_b, U_B)):
        steps.append((v_units.at[u], target, 2))
    for j in range(WIDE):
        steps.append((v_units.at[U_OUT + j], o_mlp.at[pl.ds(j * SHARE, SHARE)], 2))
    mine = lax.axis_index("dp") * SHARE
    turned = pltpu.roll(gain[...], lax.rem(D - mine, D), 1)
    for k in range(3):
        o_gain[k] = turned[k : k + 1, :SHARE]
    going = []
    waited = -1
    for i, (source, target, after) in enumerate(steps):
        if after > waited:
            coming[after].wait()
            waited = after
        going.append(pltpu.make_async_copy(source, target, sem.at[i]))
        going[-1].start()
    for copy in going:
        copy.wait()


def results(out, grad, gain, units):
    anywhere = pl.BlockSpec(memory_space=pl.ANY)
    vmem = pl.BlockSpec(memory_space=pltpu.VMEM)
    shapes = [(3, 1, SHARE), (SHARE, 3 * D), (SHARE, D), (SHARE, D), (SHARE, D)]
    shapes += [(SHARE, FF), (WIDE * SHARE, D)]
    copies = 2 + UNITS
    found = pl.pallas_call(
        results_kernel,
        out_shape=[
            jax.ShapeDtypeStruct(out.shape, BF),
            jax.ShapeDtypeStruct(grad.shape, F32),
        ]
        + [jax.ShapeDtypeStruct(shape, F32) for shape in shapes],
        in_specs=[anywhere, anywhere, vmem, anywhere],
        out_specs=[anywhere, anywhere, vmem] + [anywhere] * 6,
        scratch_shapes=[
            pltpu.VMEM(out.shape, BF),
            pltpu.VMEM(grad.shape, F32),
            pltpu.VMEM(units.shape, F32),
            pltpu.SemaphoreType.DMA((3,)),
            pltpu.SemaphoreType.DMA((copies,)),
        ],
        compiler_params=pltpu.CompilerParams(vmem_limit_bytes=64 * 2**20 - 2**16),
        name="results",
    )(out, grad, gain, units)
    return (
        found[0][None],
        found[1][None],
        jnp.transpose(found[2], (1, 0, 2)),
    ) + tuple(part[None] for part in found[3:])


def body(
    dp, blocks_in, gains, attn_qkv, attn_out, cross_a, cross_b, mlp_in, mlp_out, lengths, cotangent
):
    total = blocks_in.shape[1]
    slots = total // ROWS
    scatter = dp == NZ * NY * NC

    def low(*shape):
        return pltpu.VMEM(shape, BF)

    def full(*shape):
        return pltpu.VMEM(shape, F32)

    ring = low(RING, NC, NY, NZ * SHARE, D) if scatter else low(RING, D, D)
    dma = pltpu.SemaphoreType.DMA
    scratch = [
        low(3, D, D),
        low(D, D),
        low(D, D),
        low(D, D),
        low(FF, D),
        low(FF, D),
        full(total, D),
        full(total, D),
        low(3, total, D),
        low(3, total, D),
        low(total, D),
        low(WIDE, total, D),
        low(WIDE, total, D),
        low(2, total, D),
        low(total, D),
        low(total, D),
        low(total, D),
        low(total, D),
        full(3, total, 128),
        low(3, slots, ROWS, ROWS),
        low(UNITS, NY, NZ * SHARE, D) if scatter else low(16, 128),
        ring,
        full(2, SHARE, D) if scatter else full(8, 128),
        full(5 + NZ - 1, 8, D),
        dma((9 + WIDE,)),
        dma((2, slots)),
        dma((4, 2 * slots)),
        dma((4, 2 * slots)),
        dma((UNITS,)),
        dma((UNITS,)),
        dma((UNITS,)),
        dma((UNITS,)),
        dma((UNITS, NZ - 1)),
        dma((UNITS, NZ - 1)),
        dma((2 + NZ - 1,)),
        dma((2 + NZ - 1,)),
        dma((2,)),
        pltpu.SemaphoreType.REGULAR((2,)),
    ]
    if scatter:
        grads_shape = jax.ShapeDtypeStruct((UNITS, SHARE, D), F32)
    else:
        grads_shape = jax.ShapeDtypeStruct((UNITS, D, D), BF)
    anywhere = pl.BlockSpec(memory_space=pl.ANY)
    vmem = pl.BlockSpec(memory_space=pltpu.VMEM)
    smem = pl.BlockSpec(memory_space=pltpu.SMEM)
    out, grad, gain, units = pl.pallas_call(
        functools.partial(body_kernel, slots, scatter),
        out_shape=[
            jax.ShapeDtypeStruct((total, D), BF),
            jax.ShapeDtypeStruct((total, D), F32),
            jax.ShapeDtypeStruct((8, D), F32),
            grads_shape,
        ],
        in_specs=[anywhere, vmem] + [anywhere] * 6 + [smem, anywhere],
        out_specs=[anywhere, anywhere, vmem, anywhere],
        scratch_shapes=scratch,
        compiler_params=pltpu.CompilerParams(
            collective_id=0, has_side_effects=True, vmem_limit_bytes=64 * 2**20 - 2**16
        ),
        cost_estimate=pl.CostEstimate(
            flops=104 * 10**6 * 2 * total // 4, bytes_accessed=30 * 2**20, transcendentals=0
        ),
        name="blocks",
    )(
        blocks_in[0],
        jnp.transpose(gains, (1, 0, 2)),
        attn_qkv[0],
        attn_out[0],
        cross_a[0],
        cross_b[0],
        mlp_in[0],
        mlp_out[0],
        jnp.transpose(lengths, (1, 0, 2)),
        cotangent[0],
    )
    if scatter:
        return results(out, grad, gain, units)
    else:
        grad_gains = lax.psum_scatter(
            gain[:3][None], "dp", scatter_dimension=2, tiled=True
        )
        wide = units.astype(F32)

        def across(first, count):
            return jnp.concatenate([wide[first + j] for j in range(count)], axis=1)

        parts = tuple(
            lax.psum_scatter(part[None], "dp", scatter_dimension=1, tiled=True)
            for part in (
                across(U_QKV, 3),
                wide[U_O],
                wide[U_A],
                wide[U_B],
                across(U_IN, WIDE),
                wide[U_OUT : U_OUT + WIDE].reshape(FF, D),
            )
        )
    return (out[None], grad[None], grad_gains) + parts


def solution(mesh):
    by_rows = P("section", "dp", None)
    copied = P("section", None, None)
    return jax.shard_map(
        functools.partial(body, mesh.shape["dp"]),
        mesh=mesh,
        in_specs=(by_rows,) + (copied,) * 7 + (P(None, "dp", None), by_rows),
        out_specs=(by_rows, by_rows, P("section", None, "dp")) + (by_rows,) * 6,
        check_vma=False,
    )
```

```python
import functools
import jax
import jax.numpy as jnp
from jax import lax
from jax.experimental import pallas as pl
from jax.experimental.pallas import tpu as pltpu
from jax.sharding import PartitionSpec as P

D = 768
HEADS = 12
HEAD = 64
FF = 3072
ROWS = 256
SAMPLES = 4
PAIR = 2 * HEAD
PAIRS = HEADS // 2
PIECE = ROWS // 2
WIDE = FF // D
EPSILON = 1e-06
MESH = pl.DeviceIdType.MESH
BF = jnp.bfloat16
F32 = jnp.float32

U_A, U_B, U_IN, U_OUT, U_O, U_QKV = 0, 1, 2, 6, 10, 11
UNITS = 14
RING = 4
LAGS, LAST_LAGS = (3, 3), (2, 2)
WINDOW = 4
Z_FIRST = (U_IN + 2, U_IN + 3)
U_PARTS, PARTS = UNITS - 1, 3
NZ, NY, NC = 4, 2, 2
SHARE = D // (NZ * NY * NC)


class Item:
    def __init__(self, key, unit, half=None, part=None):
        self.key, self.unit, self.half = key, unit, half
        self.share = SHARE if part is None else SHARE // PARTS
        self.part = part or 0
        self.start = self.part * NZ * self.share
        self.landing = unit


ITEMS = UNITS + PARTS - 1 + len(Z_FIRST)

NAMES = ("x_h", "gains_h", "wqkv_h", "wo_h", "wa_h", "wb_h", "win_h", "wout_h", "lens", "cot_h")
NAMES += ("bo_h", "ig_h", "gg_h", "og_h")
NAMES += ("wqkv", "wo", "wa", "wb", "win", "wout", "res", "cot", "hid", "qkv", "mix", "up", "act")
NAMES += ("gains", "mem", "qc", "oc", "low_ff", "low_sa", "rstd", "bias")
NAMES += ("core_in", "ring", "stage", "gsum", "load_sem", "out_sem", "x_send", "x_recv")
NAMES += ("c_send", "c_recv", "y_send", "y_recv", "z_send", "z_recv", "g_send", "g_recv")
NAMES += ("stage_sem", "ready")


def nn(left, right):
    return jnp.dot(left, right, preferred_element_type=F32)


def nt(left, right):
    return lax.dot_general(left, right, (((1,), (1,)), ((), ())), preferred_element_type=F32)


def tn(left, right):
    return lax.dot_general(left, right, (((0,), (0,)), ((), ())), preferred_element_type=F32)


def norm_rows(value, gain):
    centre = jnp.mean(value, axis=-1, keepdims=True)
    centred = value - centre
    spread = jnp.mean(centred * centred, axis=-1, keepdims=True)
    scale = lax.rsqrt(spread + EPSILON)
    return centred * scale * gain, scale


def gelu_parts(u):
    phi = 0.5 * (1.0 + lax.erf(u * 0.7071067811865476))
    slope = phi + u * (jnp.exp(u * u * -0.5) * 0.3989422804014327)
    return u * phi, slope


def pair_halves(block):
    low = (lax.broadcasted_iota(jnp.int32, (1, PAIR), 1) < HEAD).astype(BF)
    return jnp.concatenate([block * low, block * (1 - low)], axis=0)


def pair_join(block):
    low = lax.broadcasted_iota(jnp.int32, (1, PAIR), 1) < HEAD
    half = block.shape[0] // 2
    return jnp.where(low, block[:half], block[half:])


def body_kernel(slots, scatter, *all_refs):
    r = dict(zip(NAMES, all_refs, strict=True))
    gains, lens = r["gains"], r["lens"]
    wqkv, wo, wa, wb, win, wout = (r[k] for k in ("wqkv", "wo", "wa", "wb", "win", "wout"))
    res, cot, hid, qkv, mix, up, act, mem = (
        r[k] for k in ("res", "cot", "hid", "qkv", "mix", "up", "act", "mem")
    )
    qc, oc, low_ff, low_sa, rstd, bias = (
        r[k] for k in ("qc", "oc", "low_ff", "low_sa", "rstd", "bias")
    )
    core_in, ring, stage, gsum = (r[k] for k in ("core_in", "ring", "stage", "gsum"))
    total = slots * ROWS

    sec = lax.axis_index("section")
    me = lax.axis_index("dp")
    across = (1 - sec, me)
    if scatter:
        core = lax.rem(me, NC)
        y = lax.rem(me // NC, NY)
        z = me // (NC * NY)
        sibling = (sec, me + 1 - 2 * core)
        beside = (sec, me + NC * (1 - 2 * y))
        along = [lax.rem(z + 1 + k, NZ) for k in range(NZ - 1)]
        along_ids = [(sec, other * (NC * NY) + y * NC + core) for other in along]
        high = z // 2
        is_end = jnp.logical_or(z == 0, z == NZ - 1)
        is_mid = jnp.logical_not(is_end)

        def at_z(other):
            return (sec, other * (NC * NY) + y * NC + core)
        partners = [across, sibling, beside] + along_ids
    else:
        partners = [across]

    barrier = pltpu.get_barrier_semaphore()
    for device in partners:
        pl.semaphore_signal(barrier, inc=1, device_id=device, device_id_type=MESH)
    pl.semaphore_wait(barrier, len(partners))

    loads = {}

    def load(name, index, pieces):
        loads[name] = [
            pltpu.make_async_copy(src, dst, r["load_sem"].at[index + i])
            for i, (src, dst) in enumerate(pieces)
        ]

    def begin(*names):
        for name in names:
            for piece in loads[name]:
                piece.start()

    def loaded(*names):
        for name in names:
            for piece in loads[name]:
                piece.wait()

    load("x", 0, [(r["x_h"], low_ff)])
    load("wqkv", 1, [(r["wqkv_h"].at[:, pl.ds(j * D, D)], wqkv.at[j]) for j in range(3)])
    load("wo", 4, [(r["wo_h"], wo)])
    load("wa", 5, [(r["wa_h"], wa)])
    load("wb", 6, [(r["wb_h"], wb)])
    load(
        "win",
        7,
        [(r["win_h"].at[:, pl.ds(j * D, D)], win.at[pl.ds(j * D, D)]) for j in range(WIDE)],
    )
    load("wout", 7 + WIDE, [(r["wout_h"], wout)])
    load("cot", 8 + WIDE, [(r["cot_h"], cot)])
    load("gains", 9 + WIDE, [(r["gains_h"], gains)])
    begin("x", "gains", "wqkv", "wo")
    gsum[...] = jnp.zeros_like(gsum)

    def rows_of(s):
        return pl.ds(pl.multiple_of(s * ROWS, ROWS), ROWS)

    def cols_of(t):
        return pl.ds(t * PAIR, PAIR)

    def x_copy(kind, piece, size=PIECE):
        src, dst = ((qc, qc), (oc, oc), (mem.at[0], low_sa), (qc, qc))[kind]
        rows = pl.ds(pl.multiple_of(piece * size, size), size)
        return pltpu.make_async_remote_copy(
            src_ref=src.at[rows],
            dst_ref=dst.at[rows],
            send_sem=r["x_send"].at[kind, piece],
            recv_sem=r["x_recv"].at[kind, piece],
            device_id=across,
            device_id_type=MESH,
        )

    def segments(which, s, axis):
        places = lax.broadcasted_iota(jnp.int32, (ROWS, ROWS), axis)
        end = jnp.int32(0)
        found = jnp.zeros((ROWS, ROWS), jnp.int32)
        for j in range(SAMPLES):
            end = end + lens[s, which, j]
            found = found + jnp.where(places >= end, 1, 0)
        return found

    def self_bias(decoder, s, turned, place):
        q_axis = 1 if turned else 0
        which = 1 if decoder else 0
        keep = segments(which, s, q_axis) == segments(which, s, 1 - q_axis)
        if decoder:
            q_at = lax.broadcasted_iota(jnp.int32, (ROWS, ROWS), q_axis)
            k_at = lax.broadcasted_iota(jnp.int32, (ROWS, ROWS), 1 - q_axis)
            keep = jnp.logical_and(keep, k_at <= q_at)
        bias[place, s] = jnp.where(keep, 0.0, -1e30).astype(BF)

    def cross_bias(s, turned, place):
        q_axis = 1 if turned else 0
        q_seg = segments(1, s, q_axis)
        k_seg = segments(0, s, 1 - q_axis)
        keep = jnp.logical_or(q_seg == k_seg, q_seg == SAMPLES)
        bias[place, s] = jnp.where(keep, 0.0, -1e30).astype(BF)

    def attend_fwd(queries, keys, values, out, rows, q_rows, mask):
        for t in range(PAIRS):
            cols = cols_of(t)
            q2 = pair_halves(queries[q_rows, cols] * HEAD ** (-0.5))
            scores = nt(q2, keys[rows, cols])
            block = mask[...].astype(F32)
            scores = scores + jnp.concatenate([block, block], axis=0)
            peak = jnp.max(scores, axis=-1, keepdims=True)
            raised = jnp.exp(scores - peak)
            level = 1.0 / jnp.sum(raised, axis=-1, keepdims=True)
            mixed = nn(raised.astype(BF), values[rows, cols]) * level
            out[q_rows, cols] = pair_join(mixed).astype(BF)

    def attend_bwd(queries, keys, values, grads, rows, mask):
        for t in range(PAIRS):
            cols = cols_of(t)
            q2 = pair_halves(queries[rows, cols] * HEAD ** (-0.5))
            k2 = keys[rows, cols]
            v2 = values[rows, cols]
            scores = nt(k2, q2)
            block = mask[...].astype(F32)
            scores = scores + jnp.concatenate([block, block], axis=1)
            peak = jnp.max(scores, axis=0, keepdims=True)
            raised = jnp.exp(scores - peak)
            probs = raised * (1.0 / jnp.sum(raised, axis=0, keepdims=True))
            g2 = pair_halves(grads[rows, cols])
            g_probs = nt(v2, g2)
            g_values = nn(probs.astype(BF), g2)
            inner = jnp.sum(g_probs * probs, axis=0, keepdims=True)
            g_scores = (probs * (g_probs - inner)).astype(BF)
            g_queries = pair_join(tn(g_scores, k2)) * HEAD ** (-0.5)
            g_keys = nn(g_scores, q2)
            queries[rows, cols] = g_queries.astype(BF)
            keys[rows, cols] = g_keys.astype(BF)
            values[rows, cols] = g_values.astype(BF)

    def norm_fwd(value, index, rows):
        normed, scale = norm_rows(value, gains[index])
        normed = normed.astype(BF)
        hid[index, rows, :] = normed
        rstd[index, rows, :] = jnp.broadcast_to(scale, (ROWS, 128))
        return normed

    def norm_bwd(grad, index, rows):
        gain = gains[index]
        flat = hid[index, rows, :].astype(F32) * (1.0 / gain)
        gsum[0, pl.ds(index, 1), :] += jnp.sum(grad * flat, axis=0, keepdims=True)
        scaled = grad * gain
        first = jnp.mean(scaled, axis=-1, keepdims=True)
        second = jnp.mean(scaled * flat, axis=-1, keepdims=True)
        cot[rows, :] += (scaled - first - flat * second) * rstd[index, rows, :][:, :1]

    def self_fwd(decoder, s):
        rows = rows_of(s)
        value = low_ff[rows, :].astype(F32)
        normed = norm_fwd(value, 0, rows)
        for j in range(3):
            qkv[j, rows, :] = nn(normed, wqkv[j]).astype(BF)
        attend_fwd(qkv.at[0], qkv.at[1], qkv.at[2], mix, rows, rows, bias.at[0, s])
        res[rows, :] = low_ff[rows, :].astype(F32) + nn(mix[rows, :], wo[...])

    def feed_fwd(index, s):
        rows = rows_of(s)
        normed = norm_fwd(res[rows, :], index, rows)
        for j in range(WIDE):
            active, slope = gelu_parts(nn(normed, win[pl.ds(j * D, D), :]))
            act[j, rows, :] = active.astype(BF)
            up[j, rows, :] = slope.astype(BF)
        out = res[rows, :]
        for j in range(WIDE):
            out = out + nn(act[j, rows, :], wout[pl.ds(j * D, D), :])
        return out

    def feed_bwd(index, s):
        rows = rows_of(s)
        low = cot[rows, :].astype(BF)
        low_ff[rows, :] = low
        for j in range(WIDE):
            g_active = nt(low, wout[pl.ds(j * D, D), :])
            up[j, rows, :] = (g_active * up[j, rows, :].astype(F32)).astype(BF)
        grad = nt(up[0, rows, :], win[pl.ds(0, D), :])
        for j in range(1, WIDE):
            grad = grad + nt(up[j, rows, :], win[pl.ds(j * D, D), :])
        norm_bwd(grad, index, rows)

    def grad_out(s):
        return pltpu.make_async_copy(
            cot.at[rows_of(s)], r["ig_h"].at[rows_of(s)], r["out_sem"].at[1, s]
        )

    def self_bwd(decoder, s, between):
        rows = rows_of(s)
        low = cot[rows, :].astype(BF)
        low_sa[rows, :] = low
        act[0, rows, :] = nt(low, wo[...]).astype(BF)
        turned = bias.at[1 if decoder else 0, s]
        attend_bwd(qkv.at[0], qkv.at[1], qkv.at[2], act.at[0], rows, turned)
        between()
        grad = nt(qkv[0, rows, :], wqkv[0])
        for j in range(1, 3):
            grad = grad + nt(qkv[j, rows, :], wqkv[j])
        norm_bwd(grad, 0, rows)
        grad_out(s).start()

    def block_out(buffer, s):
        return pltpu.make_async_copy(
            buffer.at[rows_of(s)], r["bo_h"].at[rows_of(s)], r["out_sem"].at[0, s]
        )

    place = {}

    def slot_of(u):
        return place[u] % RING

    def core_copy(u):
        return pltpu.make_async_remote_copy(
            src_ref=ring.at[slot_of(u), 1 - core],
            dst_ref=core_in.at[u],
            send_sem=r["c_send"].at[u],
            recv_sem=r["c_recv"].at[u],
            device_id=sibling,
            device_id_type=MESH,
        )

    def y_place(item, first, count=1):
        rows = pl.ds(item.start + first * item.share, count * item.share)
        if item.half is not None:
            return core_in.at[item.unit, item.half, rows]
        base = item.unit * NZ * SHARE
        return win.at[pl.ds(base + item.start + first * item.share, count * item.share)]

    def z_place(item, first, count=1):
        base = item.landing * NZ * SHARE + item.start
        return wout.at[pl.ds(base + first * item.share, count * item.share)]

    def y_copy(item, piece):
        size = NZ * item.share // 2
        rows = pl.ds(item.start + piece * size, size)
        return pltpu.make_async_remote_copy(
            src_ref=core_in.at[item.unit, 1 - y, rows],
            dst_ref=y_place(item, piece * NZ // 2, NZ // 2),
            send_sem=r["y_send"].at[item.key, piece],
            recv_sem=r["y_recv"].at[item.key, piece],
            device_id=beside,
            device_id_type=MESH,
        )

    def z_copy(item, src, dst, send, recv, to):
        return pltpu.make_async_remote_copy(
            src_ref=src,
            dst_ref=dst,
            send_sem=r["z_send"].at[item.key, send],
            recv_sem=r["z_recv"].at[item.key, recv],
            device_id=at_z(to),
            device_id_type=MESH,
        )

    def from_end(item):
        return z_copy(item, y_place(item, 1 - high, 3), z_place(item, 0, 3), 0, 0, 1 + high)

    def to_end(item):
        return z_copy(item, y_place(item, 3 * high), z_place(item, 0), 0, 0, 3 * high)

    def to_mid(item):
        return z_copy(item, z_place(item, 1), z_place(item, 3), 1, 1, 2 - high)

    def to_far(item):
        far = 3 * (1 - high)
        return z_copy(item, z_place(item, 2 * (1 - high)), z_place(item, 1), 2, 1, far)

    def whole_copy(u):
        return pltpu.make_async_copy(ring.at[slot_of(u)], r["og_h"].at[u], r["c_send"].at[u])

    def claim(units):
        for u in units:
            place[u] = len(place)
            before = [v for v in place if place[v] == place[u] - RING]
            for v in before:
                if scatter:
                    core_copy(v).wait_send()
                else:
                    whole_copy(v).wait()

    def send_unit(u):
        if scatter:
            core_copy(u).start()
        else:
            whole_copy(u).start()

    def make_unit(u, left, right):
        claim([u])
        slot = slot_of(u)

        value = tn(left[...], right[...]).astype(BF)
        if scatter:
            parts = PARTS if u == U_PARTS else 1
            share = SHARE // parts
            for d in range(NZ * NY * NC):
                dz, dy, dc = d // (NY * NC), d // NC % NY, d % NC
                for k in range(parts):
                    at = d * SHARE + k * share
                    part = value[at : at + share]
                    ring[slot, dc, dy, pl.ds((k * NZ + dz) * share, share), :] = part
        else:
            ring[slot] = value
        send_unit(u)

    def make_out_units():
        units = [U_OUT + j for j in range(WIDE)]
        claim(units)

        for j in range(WIDE):
            value = tn(act[j], low_ff[...]).astype(BF)
            if scatter:
                for d in range(NY * NC):
                    for k in range(WIDE):
                        at = (d * WIDE + k) * SHARE
                        part = value[at : at + SHARE]
                        slot = slot_of(units[k])
                        ring[slot, d % NC, d // NC, pl.ds(j * SHARE, SHARE), :] = part
            else:
                ring[slot_of(units[j])] = value
        for u in units:
            send_unit(u)

    def ready_signal():
        if scatter:
            for device in [beside] + along_ids:
                pl.semaphore_signal(r["ready"], inc=1, device_id=device, device_id_type=MESH)

    def ready_wait():
        if scatter:
            pl.semaphore_wait(r["ready"], NZ)

    def core_sum(u):
        if not scatter:
            return
        core_copy(u).wait_recv()
        for h in range(NY):
            core_in[u, h] = (
                core_in[u, h].astype(F32) + ring[slot_of(u), core, h].astype(F32)
            ).astype(BF)
        if u in Z_FIRST:
            index = Z_FIRST.index(u)
            halves = [Item(u, u, half=0), Item(UNITS + PARTS - 1 + index, u, half=1)]
            halves[1].landing = UNITS + index
            for item in halves:
                z_start(item)
            flat[u] = halves
            return
        if u == U_PARTS:
            summed.append(Item(u, u, part=0))
            summed.extend(Item(UNITS + k - 1, u, part=k) for k in range(1, PARTS))
        else:
            summed.append(Item(u, u))
        pump()

    def pump():
        while summed and len(flying) < WINDOW:
            item = summed[0]
            piece = started.get(item.key, 0)
            y_copy(item, piece).start()
            flying.append(item)
            started[item.key] = piece + 1
            if piece == 0:
                beside_now.append(item)
            else:
                summed.pop(0)

    def add_into(target, other):
        target[...] = (target[...].astype(F32) + other[...].astype(F32)).astype(BF)

    def z_start(item):
        items.append(item)

        @pl.when(is_end)
        def _():
            from_end(item).start()

        @pl.when(is_mid)
        def _():
            to_end(item).start()

    def tick():
        if not scatter:
            return
        item = beside_now.pop(0)
        for piece in range(2):
            y_copy(item, piece).wait_recv()
            flying.remove(item)
            pump()
        rows = pl.ds(item.start, NZ * item.share)
        add_into(y_place(item, 0, NZ), core_in.at[item.unit, y, rows])
        z_start(item)
        halfway.append(item)
        while len(halfway) > lags[0]:
            mid_sum(halfway.pop(0))

    def mid_add(item):
        @pl.when(is_mid)
        def _():
            from_end(item).wait_recv()
            add_into(z_place(item, 1), y_place(item, 2 - high))
            to_mid(item).start()
            add_into(z_place(item, 2 * (1 - high)), y_place(item, 3 * (1 - high)))
            to_far(item).start()

    def mid_sum(item):
        mid_add(item)
        sent.append(item)
        while len(sent) > lags[1]:
            z_sum(sent.pop(0))

    summed, flying, beside_now, halfway, sent, ended, items = [], [], [], [], [], [], []
    started, flat = {}, {}
    lags = list(LAGS)

    def stage_copy(item, slot):
        rows = pl.ds(item.part * item.share, item.share)
        return pltpu.make_async_copy(
            stage.at[slot, pl.ds(0, item.share)],
            r["og_h"].at[item.unit, rows],
            r["stage_sem"].at[slot],
        )

    def write_share(item, value):
        slot = len(ended) % 2
        if len(ended) >= 2:
            stage_copy(ended[-2], slot).wait()
        stage[slot, pl.ds(0, item.share), :] = value
        stage_copy(item, slot).start()
        ended.append(item)

    def z_total(item):
        @pl.when(is_end)
        def _():
            to_end(item).wait_recv()

        to_mid(item).wait_recv()
        value = y_place(item, z)[...].astype(F32)
        value = value + z_place(item, jnp.where(is_end, 0, 2 * high))[...].astype(F32)
        return value + z_place(item, jnp.where(is_end, 1, 3))[...].astype(F32)

    def z_sum(item):
        write_share(item, z_total(item))

    def flat_mid(u):
        if scatter:
            for item in flat[u]:
                mid_add(item)

    def flat_copy(u):
        return pltpu.make_async_remote_copy(
            src_ref=core_in.at[u, 1 - y, pl.ds(z * SHARE, SHARE)],
            dst_ref=win.at[pl.ds(u * NZ * SHARE, SHARE)],
            send_sem=r["y_send"].at[u, 0],
            recv_sem=r["y_recv"].at[u, 0],
            device_id=beside,
            device_id_type=MESH,
        )

    def flat_sum(u):
        if scatter:
            for item in flat[u]:
                y_place(item, z)[...] = z_total(item).astype(BF)
            flat_copy(u).start()

    def flat_step(step):
        for u in Z_FIRST:
            if step < 3:
                (flat_mid, flat_sum, flat_end)[step](u)

    def flat_end(u):
        if scatter:
            flat_copy(u).wait_recv()
            own = core_in[u, y, pl.ds(z * SHARE, SHARE), :].astype(F32)
            other = win[pl.ds(u * NZ * SHARE, SHARE), :].astype(F32)
            write_share(Item(u, u), own + other)

    def gain_copy(step):
        source, landing, device = (
            [(0, 3, sibling), (1, 4, beside)] + [(2, 5 + k, along_ids[k]) for k in range(NZ - 1)]
        )[step]
        return pltpu.make_async_remote_copy(
            src_ref=gsum.at[source],
            dst_ref=gsum.at[landing],
            send_sem=r["g_send"].at[step],
            recv_sem=r["g_recv"].at[step],
            device_id=device,
            device_id_type=MESH,
        )

    def gain_step(step):
        if not scatter:
            return
        if step == 0:
            gain_copy(0).start()
        elif step == 1:
            gain_copy(0).wait_recv()
            gsum[1] = gsum[0] + gsum[3]
            gain_copy(1).start()
        elif step == 2:
            gain_copy(1).wait_recv()
            gsum[2] = gsum[1] + gsum[4]
            for k in range(NZ - 1):
                gain_copy(2 + k).start()
        else:
            for k in range(NZ - 1):
                gain_copy(2 + k).wait_recv()

    def gain_write():
        return pltpu.make_async_copy(gsum.at[0], r["gg_h"], r["out_sem"].at[0, 0])

    def gain_end():
        gain_step(3)
        if scatter:
            value = gsum[2]
            for k in range(NZ - 1):
                value = value + gsum[5 + k]
            gain_copy(0).wait_send()
            gsum[0] = value
        gain_write().start()

    def finish():
        lags[:] = LAST_LAGS
        if scatter:
            tick()
        gain_end()
        while beside_now:
            tick()
        while halfway:
            mid_sum(halfway.pop(0))
        while sent:
            z_sum(sent.pop(0))
        if scatter:
            for u in place:
                if place[u] >= UNITS - RING:
                    core_copy(u).wait_send()
            for item in items:
                if item.half is None:
                    for piece in range(2):
                        y_copy(item, piece).wait_send()
            for u in Z_FIRST:
                flat_copy(u).wait_send()

            @pl.when(is_end)
            def _():
                for item in items:
                    from_end(item).wait_send()

            @pl.when(is_mid)
            def _():
                for item in items:
                    to_end(item).wait_send()
                    to_mid(item).wait_send()
                    to_far(item).wait_send()

            for step in range(1, 1 + 1 + NZ - 1):
                gain_copy(step).wait_send()
            for back in (2, 1):
                stage_copy(ended[-back], (len(ended) - back) % 2).wait()
        else:
            for u in place:
                if place[u] >= UNITS - RING:
                    whole_copy(u).wait()
        for s in range(slots):
            grad_out(s).wait()
        gain_write().wait()

    def clear():
        for found in (place, started, flat, ended, items):
            found.clear()
        lags[:] = LAGS

    def loop(count, step):
        def run(s, carry):
            step(s)
            return carry

        lax.fori_loop(0, count, run, 0)

    def encoder():
        clear()

        def masks(s):
            self_bias(False, s, False, 0)
            cross_bias(s, False, 1)
            cross_bias(s, True, 2)

        loop(slots, masks)
        loaded("x", "gains", "wqkv", "wo")
        begin("win", "wout", "wa", "wb", "cot")

        def cross(s, half):
            x_copy(0, 2 * s + half).wait_recv()
            start = pl.multiple_of(s * ROWS + half * PIECE, PIECE)
            mask = bias.at[1, s, pl.ds(half * PIECE, PIECE)]
            attend_fwd(qc, mem.at[0], mem.at[1], oc, rows_of(s), pl.ds(start, PIECE), mask)
            x_copy(1, 2 * s + half).start()

        def forward(s):
            @pl.when(s < slots)
            def _():
                self_fwd(False, s)

            @pl.when(s >= 1)
            def _():
                cross(s - 1, 1)

            @pl.when(s == 0)
            def _():
                loaded("win", "wout", "wa", "wb")

            @pl.when(s < slots)
            def _():
                rows = rows_of(s)
                out = feed_fwd(1, s)
                low_ff[rows, :] = out.astype(BF)
                block_out(low_ff, s).start()
                normed = norm_fwd(out, 2, rows)
                mem[0, rows, :] = nn(normed, wa[...]).astype(BF)
                mem[1, rows, :] = nn(normed, wb[...]).astype(BF)
                cross(s, 0)

        loop(slots + 1, forward)
        loaded("cot")
        for piece in range(2 * slots):
            x_copy(1, piece).wait_send()
        def backward(s):
            rows = rows_of(s)
            block_out(low_ff, s).wait()
            x_copy(2, s, ROWS).wait_recv()
            attend_bwd(qc, mem.at[0], mem.at[1], low_sa, rows, bias.at[2, s])
            x_copy(3, s, ROWS).start()

            grad = nt(mem[0, rows, :], wa[...]) + nt(mem[1, rows, :], wb[...])
            norm_bwd(grad, 2, rows)
            feed_bwd(1, s)

        loop(slots, backward)
        ready_signal()
        make_unit(U_IN, hid.at[1], up.at[0])
        ready_wait()
        for j in range(1, WIDE):
            make_unit(U_IN + j, hid.at[1], up.at[j])
            if j > 1:
                core_sum(U_IN + j - 2)
        core_sum(U_IN + WIDE - 2)
        core_sum(U_IN + WIDE - 1)
        make_out_units()
        tick()
        core_sum(U_OUT)
        make_unit(U_A, hid.at[2], mem.at[0])
        core_sum(U_OUT + 1)
        make_unit(U_B, hid.at[2], mem.at[1])
        core_sum(U_OUT + 2)
        core_sum(U_OUT + 3)

        def memory_units():
            core_sum(U_A)
            core_sum(U_B)
            tick()

        for s in range(slots):
            self_bwd(False, s, memory_units if s == 0 else tick)
            if s != 1:
                tick()
            flat_step(s)
        gain_step(0)
        make_unit(U_O, mix, low_sa)
        gain_step(1)
        make_unit(U_QKV, hid.at[0], qkv.at[0])
        tick()
        core_sum(U_O)
        gain_step(2)
        make_unit(U_QKV + 1, hid.at[0], qkv.at[1])
        core_sum(U_QKV)
        make_unit(U_QKV + 2, hid.at[0], qkv.at[2])
        core_sum(U_QKV + 1)
        core_sum(U_QKV + 2)
        for s in range(slots):
            x_copy(3, s, ROWS).wait_send()
        finish()

    def decoder():
        clear()
        begin("wa")

        def masks(s):
            self_bias(True, s, False, 0)
            self_bias(True, s, True, 1)

        loop(slots, masks)
        loaded("x", "gains", "wqkv", "wo")
        begin("wb", "win", "wout", "cot")
        loaded("wa")

        def first(s):
            rows = rows_of(s)
            self_fwd(True, s)
            normed = norm_fwd(res[rows, :], 1, rows)
            qc[rows, :] = nn(normed, wa[...]).astype(BF)
            x_copy(0, s).start()

        loop(slots, first)
        pieces = 2 * slots
        for piece in range(slots - 2):
            x_copy(0, piece).wait_send()
        for piece in range(slots, pieces - 1):
            x_copy(0, piece - 2).wait_send()
            x_copy(0, piece).start()
        loaded("wb", "win", "wout", "cot")

        def second(s):
            rows = rows_of(s)
            x_copy(1, 2 * s).wait_recv()
            x_copy(1, 2 * s + 1).wait_recv()
            res[rows, :] += nn(oc[rows, :], wb[...])
            low_sa[rows, :] = feed_fwd(2, s).astype(BF)
            block_out(low_sa, s).start()

            @pl.when(s == 0)
            def _():
                x_copy(0, pieces - 3).wait_send()
                x_copy(0, pieces - 1).start()

            feed_bwd(2, s)
            low = cot[rows, :].astype(BF)
            mem[1, rows, :] = low
            mem[0, rows, :] = nt(low, wb[...]).astype(BF)

            @pl.when(s == slots - 1)
            def _():
                x_copy(0, pieces - 2).wait_send()
                x_copy(0, pieces - 1).wait_send()

            x_copy(2, s, ROWS).start()

        loop(slots, second)
        ready_signal()
        make_unit(U_IN, hid.at[2], up.at[0])
        ready_wait()
        for j in range(1, WIDE):
            make_unit(U_IN + j, hid.at[2], up.at[j])
            if j > 1:
                core_sum(U_IN + j - 2)
        core_sum(U_IN + WIDE - 2)
        core_sum(U_IN + WIDE - 1)
        make_out_units()
        tick()
        core_sum(U_OUT)
        make_unit(U_B, oc, mem.at[1])
        for j in range(1, WIDE):
            core_sum(U_OUT + j)
        tick()
        core_sum(U_B)

        def third(s):
            rows = rows_of(s)
            x_copy(3, s, ROWS).wait_recv()
            block_out(low_sa, s).wait()
            norm_bwd(nt(qc[rows, :], wa[...]), 1, rows)
            self_bwd(True, s, tick)

        for s in range(slots):
            third(s)
            if s != 1:
                tick()
            flat_step(s)
        gain_step(0)
        make_unit(U_A, hid.at[1], qc)
        gain_step(1)
        make_unit(U_O, mix, low_sa)
        core_sum(U_A)
        gain_step(2)
        make_unit(U_QKV, hid.at[0], qkv.at[0])
        tick()
        core_sum(U_O)
        make_unit(U_QKV + 1, hid.at[0], qkv.at[1])
        core_sum(U_QKV)
        make_unit(U_QKV + 2, hid.at[0], qkv.at[2])
        core_sum(U_QKV + 1)
        core_sum(U_QKV + 2)
        for s in range(slots):
            x_copy(2, s, ROWS).wait_send()
        finish()

    @pl.when(sec == 0)
    def _():
        encoder()

    @pl.when(sec == 1)
    def _():
        decoder()


def results_kernel(out, grad, gain, units, o_out, o_grad, o_gain, *rest):
    o_grads = rest[:6]
    v_out, v_grad, v_units, in_sem, sem = rest[6:]
    coming = [
        pltpu.make_async_copy(a, b, in_sem.at[i])
        for i, (a, b) in enumerate(((out, v_out), (grad, v_grad), (units, v_units)))
    ]
    for copy in coming:
        copy.start()
    steps = [(v_out, o_out, 0), (v_grad, o_grad, 1)]
    o_qkv, o_o, o_a, o_b, o_in, o_mlp = o_grads
    for target, first, count in ((o_qkv, U_QKV, 3), (o_in, U_IN, WIDE)):
        for j in range(count):
            steps.append((v_units.at[first + j], target.at[:, pl.ds(j * D, D)], 2))
    for target, u in ((o_o, U_O), (o_a, U_A), (o_b, U_B)):
        steps.append((v_units.at[u], target, 2))
    for j in range(WIDE):
        steps.append((v_units.at[U_OUT + j], o_mlp.at[pl.ds(j * SHARE, SHARE)], 2))
    mine = lax.axis_index("dp") * SHARE
    turned = pltpu.roll(gain[...], lax.rem(D - mine, D), 1)
    for k in range(3):
        o_gain[k] = turned[k : k + 1, :SHARE]
    going = []
    waited = -1
    for i, (source, target, after) in enumerate(steps):
        if after > waited:
            coming[after].wait()
            waited = after
        going.append(pltpu.make_async_copy(source, target, sem.at[i]))
        going[-1].start()
    for copy in going:
        copy.wait()


def results(out, grad, gain, units):
    anywhere = pl.BlockSpec(memory_space=pl.ANY)
    vmem = pl.BlockSpec(memory_space=pltpu.VMEM)
    shapes = [(3, 1, SHARE), (SHARE, 3 * D), (SHARE, D), (SHARE, D), (SHARE, D)]
    shapes += [(SHARE, FF), (WIDE * SHARE, D)]
    copies = 2 + UNITS
    found = pl.pallas_call(
        results_kernel,
        out_shape=[
            jax.ShapeDtypeStruct(out.shape, BF),
            jax.ShapeDtypeStruct(grad.shape, F32),
        ]
        + [jax.ShapeDtypeStruct(shape, F32) for shape in shapes],
        in_specs=[anywhere, anywhere, vmem, anywhere],
        out_specs=[anywhere, anywhere, vmem] + [anywhere] * 6,
        scratch_shapes=[
            pltpu.VMEM(out.shape, BF),
            pltpu.VMEM(grad.shape, F32),
            pltpu.VMEM(units.shape, F32),
            pltpu.SemaphoreType.DMA((3,)),
            pltpu.SemaphoreType.DMA((copies,)),
        ],
        compiler_params=pltpu.CompilerParams(vmem_limit_bytes=64 * 2**20 - 2**16),
        name="results",
    )(out, grad, gain, units)
    return (
        found[0][None],
        found[1][None],
        jnp.transpose(found[2], (1, 0, 2)),
    ) + tuple(part[None] for part in found[3:])


def body(
    dp, blocks_in, gains, attn_qkv, attn_out, cross_a, cross_b, mlp_in, mlp_out, lengths, cotangent
):
    total = blocks_in.shape[1]
    slots = total // ROWS
    scatter = dp == NZ * NY * NC

    def low(*shape):
        return pltpu.VMEM(shape, BF)

    def full(*shape):
        return pltpu.VMEM(shape, F32)

    ring = low(RING, NC, NY, NZ * SHARE, D) if scatter else low(RING, D, D)
    dma = pltpu.SemaphoreType.DMA
    scratch = [
        low(3, D, D),
        low(D, D),
        low(D, D),
        low(D, D),
        low(FF, D),
        low(FF, D),
        full(total, D),
        full(total, D),
        low(3, total, D),
        low(3, total, D),
        low(total, D),
        low(WIDE, total, D),
        low(WIDE, total, D),
        full(3, 1, D),
        low(2, total, D),
        low(total, D),
        low(total, D),
        low(total, D),
        low(total, D),
        full(3, total, 128),
        low(3, slots, ROWS, ROWS),
        low(UNITS, NY, NZ * SHARE, D) if scatter else low(16, 128),
        ring,
        full(2, SHARE, D) if scatter else full(8, 128),
        full(5 + NZ - 1, 8, D),
        dma((10 + WIDE,)),
        dma((2, slots)),
        dma((4, 2 * slots)),
        dma((4, 2 * slots)),
        dma((UNITS,)),
        dma((UNITS,)),
        dma((ITEMS, 2)),
        dma((ITEMS, 2)),
        dma((ITEMS, 3)),
        dma((ITEMS, 2)),
        dma((2 + NZ - 1,)),
        dma((2 + NZ - 1,)),
        dma((2,)),
        pltpu.SemaphoreType.REGULAR,
    ]
    if scatter:
        grads_shape = jax.ShapeDtypeStruct((UNITS, SHARE, D), F32)
    else:
        grads_shape = jax.ShapeDtypeStruct((UNITS, D, D), BF)
    anywhere = pl.BlockSpec(memory_space=pl.ANY)
    smem = pl.BlockSpec(memory_space=pltpu.SMEM)
    out, grad, gain, units = pl.pallas_call(
        functools.partial(body_kernel, slots, scatter),
        out_shape=[
            jax.ShapeDtypeStruct((total, D), BF),
            jax.ShapeDtypeStruct((total, D), F32),
            jax.ShapeDtypeStruct((8, D), F32),
            grads_shape,
        ],
        in_specs=[anywhere] * 8 + [smem, anywhere],
        out_specs=[anywhere] * 4,
        scratch_shapes=scratch,
        compiler_params=pltpu.CompilerParams(
            collective_id=0, has_side_effects=True, vmem_limit_bytes=64 * 2**20 - 2**16
        ),
        cost_estimate=pl.CostEstimate(
            flops=104 * 10**6 * 2 * total // 4, bytes_accessed=30 * 2**20, transcendentals=0
        ),
        name="blocks",
    )(
        blocks_in[0],
        jnp.transpose(gains, (1, 0, 2)),
        attn_qkv[0],
        attn_out[0],
        cross_a[0],
        cross_b[0],
        mlp_in[0],
        mlp_out[0],
        jnp.transpose(lengths, (1, 0, 2)),
        cotangent[0],
    )
    if scatter:
        return results(out, grad, gain, units)
    else:
        grad_gains = lax.psum_scatter(
            gain[:3][None], "dp", scatter_dimension=2, tiled=True
        )
        wide = units.astype(F32)

        def across(first, count):
            return jnp.concatenate([wide[first + j] for j in range(count)], axis=1)

        parts = tuple(
            lax.psum_scatter(part[None], "dp", scatter_dimension=1, tiled=True)
            for part in (
                across(U_QKV, 3),
                wide[U_O],
                wide[U_A],
                wide[U_B],
                across(U_IN, WIDE),
                wide[U_OUT : U_OUT + WIDE].reshape(FF, D),
            )
        )
    return (out[None], grad[None], grad_gains) + parts


def solution(mesh):
    by_rows = P("section", "dp", None)
    copied = P("section", None, None)
    return jax.shard_map(
        functools.partial(body, mesh.shape["dp"]),
        mesh=mesh,
        in_specs=(by_rows,) + (copied,) * 7 + (P(None, "dp", None), by_rows),
        out_specs=(by_rows, by_rows, P("section", None, "dp")) + (by_rows,) * 6,
        check_vma=False,
    )
```
